32 devices in a mesh: ab: 4 (over y, x), cd: 8 (over z, core).
Axes of the slice: x: 2, y: 2, z: 4, core: 2. Of those that a mesh axis runs over, the one named last changes fastest.
Arguments:
- factors: bfloat16 [128, 128, 2048], P('ab', 'cd'), may hold values from -0.25 to 0.25
- amplitudes: float32 [256, 128, 128], P('cd', 'ab'), may hold values from -4 to 4
- driving: float32 [256, 128, 128], P('cd', 'ab'), may hold values from -8 to 8
- occ_energy: float32 [32], replicated, may hold values from -2 to -0.5
- vir_energy: float32 [128], replicated, may hold values from 0.5 to 3
Outputs:
- new_amplitudes: float32 [256, 128, 128], P('cd', 'ab')
- residual: float32 [256, 128, 128], P('cd', 'ab')
The draws below stay inside these ranges and needn't reach their ends.
All inputs are finite; a program needn't handle non-finite values.
Results may differ from the reference program's by a relative error of at most 0.0036.
Values may be sent and summed in bfloat16 or wider, within the bound.
A program may use at most 128 MiB of HBM per device.

```python
import jax
import jax.numpy as jnp
from jax import lax

VIRT = 128
AUX = 2048
NOCC = 32
ITERS = 2
OO = 256


def strengthened(array, stream_key, source, target, parts, factor):
    def block_of(position):
        return (jnp.arange(array.shape[position]) // (array.shape[position] // parts)).reshape((-1,) + (1,) * (array.ndim - 1 - position))

    first = jax.random.permutation(stream_key, parts)[block_of(target)]
    other_side = (block_of(target) + parts // 2) % parts
    return jnp.where((block_of(source) == first) | (block_of(source) == other_side), factor * array, array)


def shard_levels(rng, dims, shards, low, largest):
    gain, own = 1.0, jax.random.fold_in(rng, 6)
    for axis_at, parts in shards:
        steps = jnp.exp(jax.random.uniform(jax.random.fold_in(own, axis_at), (parts,), jnp.float32, low / len(shards), largest / len(shards)))
        gain = gain * jnp.repeat(steps, dims[axis_at] // parts).reshape([-1 if axis == axis_at else 1 for axis in range(len(dims))])
    return gain


def scatter_about(rng, shape, deviation, bound, split=(), held_as=jnp.bfloat16):
    result = jax.random.normal(rng, shape, jnp.float32) * deviation
    if len(split) > 0:
        result = shard_levels(rng, shape, split, -0.22, 0.18) * result
    return jnp.clip(result, min=-bound, max=bound).astype(held_as)


def gaussian_with(key, dims, scale, reach, pieces, heavy, held_as=jnp.bfloat16):
    array = scale * jax.random.normal(key, dims, jnp.float32)
    if pieces:
        array = array * shard_levels(key, dims, pieces, -0.22, 0.18)
    return jnp.clip(strengthened(array, jax.random.fold_in(key, 3), *heavy), -reach, reach).astype(held_as)


def setup_inputs(seed: int = 0) -> dict:
    splits = jax.random.split(jax.random.key(seed), 6)
    factors = scatter_about(splits[0], (VIRT, VIRT, AUX), ((2.0 / (VIRT * AUX ** 0.5)) ** 0.5), 0.25, ((0, 4), (1, 8)))
    amplitudes = gaussian_with(splits[1], (OO, VIRT, VIRT), 0.5, 4.0, ((0, 8), (1, 4)), (2, 0, 8, 2.0), jnp.float32)
    driving = scatter_about(splits[2], (OO, VIRT, VIRT), 2.0, 8.0, ((0, 8), (1, 4)), jnp.float32)
    occ_energy = jnp.clip(jax.random.uniform(splits[3], (NOCC,), jnp.float32, -2.0, -0.5), -2.0, -0.5)
    vir_energy = jnp.clip(jax.random.uniform(splits[4], (VIRT,), jnp.float32, 0.5, 3.0), 0.5, 3.0)
    return {"factors": factors, "amplitudes": amplitudes, "driving": driving, "occ_energy": occ_energy, "vir_energy": vir_energy}


def reference(factors, amplitudes, driving, occ_energy, vir_energy):
    n_occ = occ_energy.shape[0]
    pairs = amplitudes.shape[0]
    virtuals = amplitudes.shape[1]
    aux_width = factors.shape[2]
    row_ids = lax.iota(jnp.int32, pairs)
    occ_pair = occ_energy[row_ids // n_occ] + occ_energy[row_ids % n_occ]
    denominator = vir_energy[None, :, None] + vir_energy[None, None, :] - occ_pair[:, None, None]
    right_flat = factors.reshape(virtuals * virtuals, aux_width)
    current = amplitudes
    residual = amplitudes
    for step in range(ITERS):
        rounded = current.astype(jnp.bfloat16).astype(jnp.float32)

        def one_virtual(left):
            tile = lax.dot_general(left, right_flat, (((1,), (1,)), ((), ())), preferred_element_type=jnp.float32)
            tile = tile.astype(jnp.bfloat16).astype(jnp.float32).reshape(virtuals, virtuals, virtuals)
            return jnp.einsum('icd,cbd->ib', rounded, tile)

        stacked = lax.map(one_virtual, factors)
        ladder = jnp.transpose(stacked, (1, 0, 2))
        symmetric = 0.5 * (ladder + jnp.transpose(ladder, (0, 2, 1)))
        residual = driving + denominator * current + symmetric
        current = current - residual / denominator
    return current, residual
```

```python
import functools

import jax
import jax.numpy as jnp
from jax import lax
from jax.experimental import pallas as pl
from jax.experimental.pallas import tpu as pltpu
from jax.sharding import PartitionSpec as P

ITERS = 2
MESH = pl.DeviceIdType.MESH


def local_general(factors, amplitudes, driving, occ_energy, vir_energy):
    rows = amplitudes.shape[0]
    a_local = amplitudes.shape[1]
    virtuals = amplitudes.shape[2]
    aux_width = factors.shape[2]
    n_cd = lax.axis_size("cd")
    d_local = factors.shape[1]
    pairs = rows * n_cd
    cd_index = lax.axis_index("cd")
    ab_index = lax.axis_index("ab")
    left_rows = lax.all_gather(factors, "cd", axis=1, tiled=True)
    left_flat = left_rows.reshape(a_local * virtuals, aux_width)
    piece = lax.all_gather(factors, "ab", axis=0, tiled=True)
    count = piece.shape[0]
    product = lax.dot_general(
        left_flat,
        piece.reshape(count * d_local, aux_width),
        (((1,), (1,)), ((), ())),
        preferred_element_type=jnp.float32,
    )
    product = product.reshape(a_local, virtuals, count, d_local)
    tiles = (
        product.transpose(0, 2, 3, 1)
        .reshape(a_local, count, d_local * virtuals)
        .astype(jnp.bfloat16)
    )
    tiles = tiles.reshape(a_local * virtuals, d_local * virtuals)
    n_occ = occ_energy.shape[0]
    row_ids = cd_index * rows + lax.iota(jnp.int32, rows)
    orbitals = lax.iota(jnp.int32, n_occ)
    first_hot = (row_ids[:, None] // n_occ == orbitals[None, :]).astype(jnp.float32)
    second_hot = (row_ids[:, None] % n_occ == orbitals[None, :]).astype(jnp.float32)
    occ_pair = jnp.sum((first_hot + second_hot) * occ_energy[None, :], axis=1)
    vir_rows = lax.dynamic_slice_in_dim(vir_energy, ab_index * a_local, a_local)
    denominator = vir_rows[None, :, None] + vir_energy[None, None, :] - occ_pair[:, None, None]
    current = amplitudes
    residual = amplitudes
    for step in range(ITERS):
        rounded = current.astype(jnp.bfloat16)
        own_block = lax.all_to_all(
            rounded.transpose(2, 1, 0), "cd", split_axis=0, concat_axis=2, tiled=True
        )
        gathered = lax.all_gather(own_block, "ab", axis=1, tiled=True)
        flat_amps = gathered.reshape(d_local * virtuals, pairs)
        summed = lax.psum_scatter(
            lax.dot_general(
                flat_amps, tiles, (((0,), (1,)), ((), ())), preferred_element_type=jnp.float32
            ),
            "cd",
            scatter_dimension=0,
            tiled=True,
        ).reshape(rows, a_local, virtuals)
        mirrored = lax.all_to_all(summed, "ab", split_axis=2, concat_axis=1, tiled=True).transpose(
            0, 2, 1
        )
        symmetric = 0.5 * (summed + mirrored)
        residual = driving + denominator * current + symmetric
        current = current - residual / denominator
    return (current, residual)


def integral_kernel(virtuals, d_local, left_ref, right_ref, out_ref):
    a_step = left_ref.shape[0] // virtuals
    product = lax.dot_general(
        left_ref[...], right_ref[...], (((1,), (1,)), ((), ())), preferred_element_type=jnp.float32
    ).astype(jnp.bfloat16)
    for a in range(a_step):
        for d in range(d_local):
            out_ref[d * virtuals:(d + 1) * virtuals, a * virtuals:(a + 1) * virtuals] = product[
                a * virtuals:(a + 1) * virtuals, d * virtuals:(d + 1) * virtuals
            ]


def integral_tiles(left, right, virtuals, d_local):
    a_step = 2
    rows, depth = left.shape
    a_local = rows // virtuals
    return pl.pallas_call(
        functools.partial(integral_kernel, virtuals, d_local),
        grid=(a_local // a_step,),
        in_specs=[
            pl.BlockSpec((a_step * virtuals, depth), lambda i: (i, 0)),
            pl.BlockSpec(right.shape, lambda i: (0, 0)),
        ],
        out_specs=pl.BlockSpec((d_local * virtuals, a_step * virtuals), lambda i: (0, i)),
        out_shape=jax.ShapeDtypeStruct((d_local * virtuals, a_local * virtuals), jnp.bfloat16),
        compiler_params=pltpu.CompilerParams(vmem_limit_bytes=48 * 2**20),
        cost_estimate=pl.CostEstimate(
            flops=2 * rows * right.shape[0] * depth,
            bytes_accessed=2 * (rows * depth + right.size + rows * right.shape[0]),
            transcendentals=0,
        ),
    )(left, right)


def ladder_kernel(
    n_ab, n_cd, chunks, v_ref, sym_amp_ref, sym_drv_ref, den_ref, out_ref,
    amps, part, pair_in, pair_out, arrived, state, packed,
    amp_send, amp_recv, amp_local, pair_send, pair_recv, red_send, red_recv,
):
    ab = lax.axis_index("ab")
    cd = lax.axis_index("cd")
    n_z = n_cd // 2
    z = cd // 2
    h = cd % 2
    rows, width = sym_amp_ref.shape
    depth = v_ref.shape[0]
    cols = width // chunks

    barrier = pltpu.get_barrier_semaphore()
    for i in range(n_ab):
        for j in range(n_cd):
            @pl.when(jnp.logical_not((ab == i) & (cd == j)))
            def _():
                pl.semaphore_signal(barrier, inc=1, device_id=(i, j), device_id_type=MESH)
    pl.semaphore_wait(barrier, n_ab * n_cd - 1)

    state[...] = sym_amp_ref[...]

    def amp_copy(it, i, k):
        return pltpu.make_async_remote_copy(
            src_ref=packed.at[it, :, pl.ds(k * depth, depth)],
            dst_ref=amps.at[it, pl.ds(cd * rows, rows), :],
            send_sem=amp_send.at[it, i, k],
            recv_sem=amp_recv.at[it, cd],
            device_id=(i, 2 * ab + k),
            device_id_type=MESH,
        )

    def amp_local_copy(it, k):
        return pltpu.make_async_copy(
            packed.at[it, :, pl.ds(k * depth, depth)],
            amps.at[it, pl.ds(cd * rows, rows), :],
            amp_local.at[it],
        )

    def amp_arrival(it, j):
        return pltpu.make_async_remote_copy(
            src_ref=packed.at[it, :, pl.ds(0, depth)],
            dst_ref=amps.at[it, pl.ds(j * rows, rows), :],
            send_sem=amp_send.at[it, 0, 0],
            recv_sem=amp_recv.at[it, j],
            device_id=(ab, 1 - h + 2 * z),
            device_id_type=MESH,
        )

    def pair_copy(it, c):
        return pltpu.make_async_remote_copy(
            src_ref=part.at[it, pl.ds(pl.multiple_of((1 - h) * n_z, n_z), n_z), :, pl.ds(c * cols, cols)],
            dst_ref=pair_in.at[it, :, :, pl.ds(c * cols, cols)],
            send_sem=pair_send.at[it, c],
            recv_sem=pair_recv.at[it, c],
            device_id=(ab, 2 * z + 1 - h),
            device_id_type=MESH,
        )

    def red_copy(it, c, s):
        to = lax.rem(z + s, n_z)
        return pltpu.make_async_remote_copy(
            src_ref=pair_out.at[it, to, :, pl.ds(c * cols, cols)],
            dst_ref=arrived.at[it, s - 1, :, pl.ds(c * cols, cols)],
            send_sem=red_send.at[it, c, s - 1],
            recv_sem=red_recv.at[it, c, s - 1],
            device_id=(ab, 2 * to + h),
            device_id_type=MESH,
        )

    for it in range(ITERS):
        packed[it] = state[...].astype(jnp.bfloat16)
        for i in range(n_ab):
            for k in range(2):
                mine = (ab == i) & (cd == 2 * ab + k)

                @pl.when(jnp.logical_not(mine))
                def _():
                    amp_copy(it, i, k).start()

                @pl.when(mine)
                def _():
                    amp_local_copy(it, k).start()
                    amp_local_copy(it, k).wait()
        for j in range(n_cd):
            @pl.when(jnp.logical_not((ab == z) & (cd == j)))
            def _():
                amp_arrival(it, j).wait_recv()

        def reduce_chunk(c):
            pair_copy(it, c).wait_recv()
            at = pl.ds(c * cols, cols)
            total = part[it, pl.ds(pl.multiple_of(h * n_z, n_z), n_z), :, at].astype(jnp.float32) + pair_in[
                it, :, :, at
            ].astype(jnp.float32)
            pair_out[it, :, :, at] = total.astype(jnp.bfloat16)
            for s in range(1, n_z):
                red_copy(it, c, s).start()

        for c in range(chunks):
            value = jnp.dot(
                amps[it], v_ref[:, c * cols:(c + 1) * cols], preferred_element_type=jnp.float32
            ).astype(jnp.bfloat16)
            for j in range(n_cd):
                part[it, (j % 2) * n_z + j // 2, :, c * cols:(c + 1) * cols] = value[j * rows:(j + 1) * rows]
            pair_copy(it, c).start()
            if c > 0:
                reduce_chunk(c - 1)
        reduce_chunk(chunks - 1)
        for c in range(chunks):
            for s in range(1, n_z):
                red_copy(it, c, s).wait_recv()
            at = pl.ds(c * cols, cols)
            total = pair_out[it, z, :, at].astype(jnp.float32)
            for s in range(1, n_z):
                total = total + arrived[it, s - 1, :, at].astype(jnp.float32)
            out_ref[it, :, at] = total
            if it + 1 < ITERS:
                old = state[:, at]
                den = den_ref[:, at]
                state[:, at] = old - (sym_drv_ref[:, at] + den * old + total) / den
    for it in range(ITERS):
        for i in range(n_ab):
            for k in range(2):
                @pl.when(jnp.logical_not((ab == i) & (cd == 2 * ab + k)))
                def _():
                    amp_copy(it, i, k).wait_send()
        for c in range(chunks):
            pair_copy(it, c).wait_send()
            for s in range(1, n_z):
                red_copy(it, c, s).wait_send()


def ladders(tiles, sym_amp, sym_drv, den, n_ab, n_cd):
    rows, width = sym_amp.shape
    depth = tiles.shape[0]
    n_z = n_cd // 2
    chunks = 4
    vmem = pl.BlockSpec(memory_space=pltpu.VMEM)
    dma = pltpu.SemaphoreType.DMA
    return pl.pallas_call(
        functools.partial(ladder_kernel, n_ab, n_cd, chunks),
        out_shape=jax.ShapeDtypeStruct((ITERS, rows, width), jnp.float32),
        in_specs=[vmem] * 4,
        out_specs=vmem,
        scratch_shapes=[
            pltpu.VMEM((ITERS, n_cd * rows, depth), jnp.bfloat16),
            pltpu.VMEM((ITERS, n_cd, rows, width), jnp.bfloat16),
            pltpu.VMEM((ITERS, n_z, rows, width), jnp.bfloat16),
            pltpu.VMEM((ITERS, n_z, rows, width), jnp.bfloat16),
            pltpu.VMEM((ITERS, n_z - 1, rows, width), jnp.bfloat16),
            pltpu.VMEM((rows, width), jnp.float32),
            pltpu.VMEM((ITERS, rows, width), jnp.bfloat16),
            dma((ITERS, n_ab, 2)),
            dma((ITERS, n_cd)),
            dma((ITERS,)),
            dma((ITERS, chunks)),
            dma((ITERS, chunks)),
            dma((ITERS, chunks, n_z - 1)),
            dma((ITERS, chunks, n_z - 1)),
        ],
        compiler_params=pltpu.CompilerParams(
            collective_id=0, has_side_effects=True, vmem_limit_bytes=52 * 2**20
        ),
        cost_estimate=pl.CostEstimate(
            flops=2 * ITERS * n_cd * rows * depth * width,
            bytes_accessed=tiles.size * 2,
            transcendentals=0,
        ),
    )(tiles, sym_amp, sym_drv, den)


def local_ladder(factors, amplitudes, driving, occ_energy, vir_energy):
    rows, a_local, virtuals = amplitudes.shape
    aux_width = factors.shape[2]
    d_local = factors.shape[1]
    n_ab = lax.axis_size("ab")
    n_cd = lax.axis_size("cd")
    cd_index = lax.axis_index("cd")
    ab_index = lax.axis_index("ab")
    left = lax.all_gather(factors, "cd", axis=1, tiled=True).reshape(a_local * virtuals, aux_width)
    right = lax.all_gather(factors.transpose(1, 0, 2), "ab", axis=1, tiled=True)
    right = right.reshape(d_local * virtuals, aux_width)

    both = jnp.concatenate([amplitudes, driving], axis=0)
    swapped = lax.all_to_all(both, "ab", split_axis=2, concat_axis=1, tiled=True).transpose(0, 2, 1)
    symmetric = (0.5 * (both + swapped)).reshape(2, rows, a_local * virtuals)

    n_occ = occ_energy.shape[0]
    row_ids = cd_index * rows + lax.iota(jnp.int32, rows)
    orbitals = lax.iota(jnp.int32, n_occ)
    first_hot = (row_ids[:, None] // n_occ == orbitals[None, :]).astype(jnp.float32)
    second_hot = (row_ids[:, None] % n_occ == orbitals[None, :]).astype(jnp.float32)
    occ_pair = jnp.sum((first_hot + second_hot) * occ_energy[None, :], axis=1)
    vir_rows = lax.dynamic_slice_in_dim(vir_energy, ab_index * a_local, a_local)
    denominator = vir_rows[None, :, None] + vir_energy[None, None, :] - occ_pair[:, None, None]

    tiles = integral_tiles(left, right, virtuals, d_local)
    sums = ladders(
        tiles, symmetric[0], symmetric[1], denominator.reshape(rows, a_local * virtuals), n_ab, n_cd
    ).reshape(ITERS, rows, a_local, virtuals)
    current = amplitudes
    residual = amplitudes
    for step in range(ITERS):
        residual = driving + denominator * current + sums[step]
        current = current - residual / denominator
    return (current, residual)


def solution(mesh):
    placed = (P("ab", "cd", None), P("cd", "ab", None), P("cd", "ab", None), P(), P())

    def local(factors, amplitudes, driving, occ_energy, vir_energy):
        rows, a_local, virtuals = amplitudes.shape
        paired = a_local == 2 * factors.shape[1] and mesh.shape["cd"] == 2 * mesh.shape["ab"]
        aligned = rows % 16 == 0 and virtuals % 128 == 0 and a_local % 8 == 0
        form = local_ladder if paired and aligned else local_general
        return form(factors, amplitudes, driving, occ_energy, vir_energy)

    return jax.shard_map(
        local,
        mesh=mesh,
        in_specs=placed,
        out_specs=(P("cd", "ab", None), P("cd", "ab", None)),
        check_vma=False,
    )
```

```python
import functools

import jax
import jax.numpy as jnp
from jax import lax
from jax.experimental import pallas as pl
from jax.experimental.pallas import tpu as pltpu
from jax.sharding import PartitionSpec as P

ITERS = 2
MESH = pl.DeviceIdType.MESH


def local_general(factors, amplitudes, driving, occ_energy, vir_energy):
    rows = amplitudes.shape[0]
    a_local = amplitudes.shape[1]
    virtuals = amplitudes.shape[2]
    aux_width = factors.shape[2]
    n_cd = lax.axis_size("cd")
    d_local = factors.shape[1]
    pairs = rows * n_cd
    cd_index = lax.axis_index("cd")
    ab_index = lax.axis_index("ab")
    left_rows = lax.all_gather(factors, "cd", axis=1, tiled=True)
    left_flat = left_rows.reshape(a_local * virtuals, aux_width)
    piece = lax.all_gather(factors, "ab", axis=0, tiled=True)
    count = piece.shape[0]
    product = lax.dot_general(
        left_flat,
        piece.reshape(count * d_local, aux_width),
        (((1,), (1,)), ((), ())),
        preferred_element_type=jnp.float32,
    )
    product = product.reshape(a_local, virtuals, count, d_local)
    tiles = (
        product.transpose(0, 2, 3, 1)
        .reshape(a_local, count, d_local * virtuals)
        .astype(jnp.bfloat16)
    )
    tiles = tiles.reshape(a_local * virtuals, d_local * virtuals)
    n_occ = occ_energy.shape[0]
    row_ids = cd_index * rows + lax.iota(jnp.int32, rows)
    orbitals = lax.iota(jnp.int32, n_occ)
    first_hot = (row_ids[:, None] // n_occ == orbitals[None, :]).astype(jnp.float32)
    second_hot = (row_ids[:, None] % n_occ == orbitals[None, :]).astype(jnp.float32)
    occ_pair = jnp.sum((first_hot + second_hot) * occ_energy[None, :], axis=1)
    vir_rows = lax.dynamic_slice_in_dim(vir_energy, ab_index * a_local, a_local)
    denominator = vir_rows[None, :, None] + vir_energy[None, None, :] - occ_pair[:, None, None]
    current = amplitudes
    residual = amplitudes
    for step in range(ITERS):
        rounded = current.astype(jnp.bfloat16)
        own_block = lax.all_to_all(
            rounded.transpose(2, 1, 0), "cd", split_axis=0, concat_axis=2, tiled=True
        )
        gathered = lax.all_gather(own_block, "ab", axis=1, tiled=True)
        flat_amps = gathered.reshape(d_local * virtuals, pairs)
        summed = lax.psum_scatter(
            lax.dot_general(
                flat_amps, tiles, (((0,), (1,)), ((), ())), preferred_element_type=jnp.float32
            ),
            "cd",
            scatter_dimension=0,
            tiled=True,
        ).reshape(rows, a_local, virtuals)
        mirrored = lax.all_to_all(summed, "ab", split_axis=2, concat_axis=1, tiled=True).transpose(
            0, 2, 1
        )
        symmetric = 0.5 * (summed + mirrored)
        residual = driving + denominator * current + symmetric
        current = current - residual / denominator
    return (current, residual)


def integral_kernel(virtuals, d_local, left_ref, right_ref, out_ref):
    a_step = left_ref.shape[0] // virtuals
    product = lax.dot_general(
        left_ref[...], right_ref[...], (((1,), (1,)), ((), ())), preferred_element_type=jnp.float32
    ).astype(jnp.bfloat16)
    for a in range(a_step):
        for d in range(d_local):
            out_ref[d * virtuals:(d + 1) * virtuals, a * virtuals:(a + 1) * virtuals] = product[
                a * virtuals:(a + 1) * virtuals, d * virtuals:(d + 1) * virtuals
            ]


def integral_tiles(left, right, virtuals, d_local):
    a_step = 2
    rows, depth = left.shape
    a_local = rows // virtuals
    return pl.pallas_call(
        functools.partial(integral_kernel, virtuals, d_local),
        grid=(a_local // a_step,),
        in_specs=[
            pl.BlockSpec((a_step * virtuals, depth), lambda i: (i, 0)),
            pl.BlockSpec(right.shape, lambda i: (0, 0)),
        ],
        out_specs=pl.BlockSpec((d_local * virtuals, a_step * virtuals), lambda i: (0, i)),
        out_shape=jax.ShapeDtypeStruct((d_local * virtuals, a_local * virtuals), jnp.bfloat16),
        compiler_params=pltpu.CompilerParams(vmem_limit_bytes=48 * 2**20),
        cost_estimate=pl.CostEstimate(
            flops=2 * rows * right.shape[0] * depth,
            bytes_accessed=2 * (rows * depth + right.size + rows * right.shape[0]),
            transcendentals=0,
        ),
    )(left, right)


def ladder_kernel(
    n_ab, n_cd, chunks, v_ref, sym_amp_ref, sym_drv_ref, den_ref, out_ref,
    amps, part, pair_in, pair_out, arrived, state, relay,
    layer_send, layer_recv, amp_send, amp_recv, amp_local, pair_send, pair_recv, red_send, red_recv,
):
    ab = lax.axis_index("ab")
    cd = lax.axis_index("cd")
    n_z = n_cd // 2
    z = cd // 2
    h = cd % 2
    rows, width = sym_amp_ref.shape
    depth = v_ref.shape[0]
    cols = width // chunks

    barrier = pltpu.get_barrier_semaphore()
    for i in range(n_ab):
        for j in range(n_cd):
            @pl.when(jnp.logical_not((ab == i) & (cd == j)))
            def _():
                pl.semaphore_signal(barrier, inc=1, device_id=(i, j), device_id_type=MESH)
    pl.semaphore_wait(barrier, n_ab * n_cd - 1)

    state[...] = sym_amp_ref[...]

    def layer_copy(it, s):
        return pltpu.make_async_remote_copy(
            src_ref=relay.at[it, ab],
            dst_ref=relay.at[it, ab],
            send_sem=layer_send.at[it, s - 1],
            recv_sem=layer_recv.at[it, s - 1],
            device_id=(lax.rem(ab + s, n_ab), cd),
            device_id_type=MESH,
        )

    def slot(s):
        return lax.rem(ab + n_ab - s, n_ab)

    def amp_copy(it, s, k):
        return pltpu.make_async_remote_copy(
            src_ref=relay.at[it, slot(s), :, pl.ds(k * depth, depth)],
            dst_ref=amps.at[it, pl.ds(cd * rows, rows), :],
            send_sem=amp_send.at[it, s, k],
            recv_sem=amp_recv.at[it, cd],
            device_id=(ab, 2 * slot(s) + k),
            device_id_type=MESH,
        )

    def amp_local_copy(it, s, k):
        return pltpu.make_async_copy(
            relay.at[it, slot(s), :, pl.ds(k * depth, depth)],
            amps.at[it, pl.ds(cd * rows, rows), :],
            amp_local.at[it],
        )

    def amp_arrival(it, j):
        return pltpu.make_async_remote_copy(
            src_ref=relay.at[it, 0, :, pl.ds(0, depth)],
            dst_ref=amps.at[it, pl.ds(j * rows, rows), :],
            send_sem=amp_send.at[it, 0, 0],
            recv_sem=amp_recv.at[it, j],
            device_id=(ab, 1 - h + 2 * z),
            device_id_type=MESH,
        )

    def pair_copy(it, c):
        return pltpu.make_async_remote_copy(
            src_ref=part.at[it, pl.ds(pl.multiple_of((1 - h) * n_z, n_z), n_z), :, pl.ds(c * cols, cols)],
            dst_ref=pair_in.at[it, :, :, pl.ds(c * cols, cols)],
            send_sem=pair_send.at[it, c],
            recv_sem=pair_recv.at[it, c],
            device_id=(ab, 2 * z + 1 - h),
            device_id_type=MESH,
        )

    def red_copy(it, c, s):
        to = lax.rem(z + s, n_z)
        return pltpu.make_async_remote_copy(
            src_ref=pair_out.at[it, to, :, pl.ds(c * cols, cols)],
            dst_ref=arrived.at[it, s - 1, :, pl.ds(c * cols, cols)],
            send_sem=red_send.at[it, c, s - 1],
            recv_sem=red_recv.at[it, c, s - 1],
            device_id=(ab, 2 * to + h),
            device_id_type=MESH,
        )

    for it in range(ITERS):
        relay[it, ab] = state[...].astype(jnp.bfloat16)
        for s in range(1, n_ab):
            layer_copy(it, s).start()
        for s in range(n_ab):
            if s > 0:
                layer_copy(it, s).wait_recv()
            for k in range(2):
                mine = cd == 2 * slot(s) + k

                @pl.when(jnp.logical_not(mine))
                def _():
                    amp_copy(it, s, k).start()

                @pl.when(mine)
                def _():
                    amp_local_copy(it, s, k).start()
                    amp_local_copy(it, s, k).wait()
        for j in range(n_cd):
            @pl.when(cd != j)
            def _():
                amp_arrival(it, j).wait_recv()

        def reduce_chunk(c):
            pair_copy(it, c).wait_recv()
            at = pl.ds(c * cols, cols)
            total = part[it, pl.ds(pl.multiple_of(h * n_z, n_z), n_z), :, at].astype(jnp.float32) + pair_in[
                it, :, :, at
            ].astype(jnp.float32)
            pair_out[it, :, :, at] = total.astype(jnp.bfloat16)
            for s in range(1, n_z):
                red_copy(it, c, s).start()

        for c in range(chunks):
            value = jnp.dot(
                amps[it], v_ref[:, c * cols:(c + 1) * cols], preferred_element_type=jnp.float32
            ).astype(jnp.bfloat16)
            for j in range(n_cd):
                part[it, (j % 2) * n_z + j // 2, :, c * cols:(c + 1) * cols] = value[j * rows:(j + 1) * rows]
            pair_copy(it, c).start()
            if c > 0:
                reduce_chunk(c - 1)
        reduce_chunk(chunks - 1)
        for c in range(chunks):
            for s in range(1, n_z):
                red_copy(it, c, s).wait_recv()
            at = pl.ds(c * cols, cols)
            total = pair_out[it, z, :, at].astype(jnp.float32)
            for s in range(1, n_z):
                total = total + arrived[it, s - 1, :, at].astype(jnp.float32)
            out_ref[it, :, at] = total
            if it + 1 < ITERS:
                old = state[:, at]
                den = den_ref[:, at]
                state[:, at] = old - (sym_drv_ref[:, at] + den * old + total) / den
    for it in range(ITERS):
        for s in range(n_ab):
            if s > 0:
                layer_copy(it, s).wait_send()
            for k in range(2):
                @pl.when(cd != 2 * slot(s) + k)
                def _():
                    amp_copy(it, s, k).wait_send()
        for c in range(chunks):
            pair_copy(it, c).wait_send()
            for s in range(1, n_z):
                red_copy(it, c, s).wait_send()


def ladders(tiles, sym_amp, sym_drv, den, n_ab, n_cd):
    rows, width = sym_amp.shape
    depth = tiles.shape[0]
    n_z = n_cd // 2
    chunks = 4
    vmem = pl.BlockSpec(memory_space=pltpu.VMEM)
    dma = pltpu.SemaphoreType.DMA
    return pl.pallas_call(
        functools.partial(ladder_kernel, n_ab, n_cd, chunks),
        out_shape=jax.ShapeDtypeStruct((ITERS, rows, width), jnp.float32),
        in_specs=[vmem] * 4,
        out_specs=vmem,
        scratch_shapes=[
            pltpu.VMEM((ITERS, n_cd * rows, depth), jnp.bfloat16),
            pltpu.VMEM((ITERS, n_cd, rows, width), jnp.bfloat16),
            pltpu.VMEM((ITERS, n_z, rows, width), jnp.bfloat16),
            pltpu.VMEM((ITERS, n_z, rows, width), jnp.bfloat16),
            pltpu.VMEM((ITERS, n_z - 1, rows, width), jnp.bfloat16),
            pltpu.VMEM((rows, width), jnp.float32),
            pltpu.VMEM((ITERS, n_ab, rows, width), jnp.bfloat16),
            dma((ITERS, n_ab - 1)),
            dma((ITERS, n_ab - 1)),
            dma((ITERS, n_ab, 2)),
            dma((ITERS, n_cd)),
            dma((ITERS,)),
            dma((ITERS, chunks)),
            dma((ITERS, chunks)),
            dma((ITERS, chunks, n_z - 1)),
            dma((ITERS, chunks, n_z - 1)),
        ],
        compiler_params=pltpu.CompilerParams(
            collective_id=0, has_side_effects=True, vmem_limit_bytes=52 * 2**20
        ),
        cost_estimate=pl.CostEstimate(
            flops=2 * ITERS * n_cd * rows * depth * width,
            bytes_accessed=tiles.size * 2,
            transcendentals=0,
        ),
    )(tiles, sym_amp, sym_drv, den)


def local_ladder(factors, amplitudes, driving, occ_energy, vir_energy):
    rows, a_local, virtuals = amplitudes.shape
    aux_width = factors.shape[2]
    d_local = factors.shape[1]
    n_ab = lax.axis_size("ab")
    n_cd = lax.axis_size("cd")
    cd_index = lax.axis_index("cd")
    ab_index = lax.axis_index("ab")
    left = lax.all_gather(factors, "cd", axis=1, tiled=True).reshape(a_local * virtuals, aux_width)
    own = factors.transpose(1, 0, 2)
    right = jnp.zeros((d_local, virtuals, aux_width), factors.dtype)
    for s in range(n_ab):
        block = lax.ppermute(own, "ab", [(i, i ^ s) for i in range(n_ab)]) if s else own
        right = lax.dynamic_update_slice_in_dim(right, block, (ab_index ^ s) * a_local, axis=1)
    right = right.reshape(d_local * virtuals, aux_width)

    both = jnp.concatenate([amplitudes, driving], axis=0)
    swapped = lax.all_to_all(both, "ab", split_axis=2, concat_axis=1, tiled=True).transpose(0, 2, 1)
    symmetric = (0.5 * (both + swapped)).reshape(2, rows, a_local * virtuals)

    n_occ = occ_energy.shape[0]
    row_ids = cd_index * rows + lax.iota(jnp.int32, rows)
    orbitals = lax.iota(jnp.int32, n_occ)
    first_hot = (row_ids[:, None] // n_occ == orbitals[None, :]).astype(jnp.float32)
    second_hot = (row_ids[:, None] % n_occ == orbitals[None, :]).astype(jnp.float32)
    occ_pair = jnp.sum((first_hot + second_hot) * occ_energy[None, :], axis=1)
    vir_rows = lax.dynamic_slice_in_dim(vir_energy, ab_index * a_local, a_local)
    denominator = vir_rows[None, :, None] + vir_energy[None, None, :] - occ_pair[:, None, None]

    tiles = integral_tiles(left, right, virtuals, d_local)
    sums = ladders(
        tiles, symmetric[0], symmetric[1], denominator.reshape(rows, a_local * virtuals), n_ab, n_cd
    ).reshape(ITERS, rows, a_local, virtuals)
    current = amplitudes
    residual = amplitudes
    for step in range(ITERS):
        residual = driving + denominator * current + sums[step]
        current = current - residual / denominator
    return (current, residual)


def solution(mesh):
    placed = (P("ab", "cd", None), P("cd", "ab", None), P("cd", "ab", None), P(), P())

    def local(factors, amplitudes, driving, occ_energy, vir_energy):
        rows, a_local, virtuals = amplitudes.shape
        paired = a_local == 2 * factors.shape[1] and mesh.shape["cd"] == 2 * mesh.shape["ab"]
        paired = paired and mesh.shape["ab"] & (mesh.shape["ab"] - 1) == 0
        aligned = rows % 16 == 0 and virtuals % 128 == 0 and a_local % 8 == 0
        form = local_ladder if paired and aligned else local_general
        return form(factors, amplitudes, driving, occ_energy, vir_energy)

    return jax.shard_map(
        local,
        mesh=mesh,
        in_specs=placed,
        out_specs=(P("cd", "ab", None), P("cd", "ab", None)),
        check_vma=False,
    )
```
